32 devices in a mesh: dp: 8 (over y, x, core), mp: 4 (over z).
Axes of the slice: x: 2, y: 2, z: 4, core: 2. Of those that a mesh axis runs over, the one named last changes fastest.
Arguments:
- gradients: bfloat16 [8, 40, 512, 512], P('dp', 'mp'), may hold values from -16 to 16
- factor_state: float32 [4, 8, 2, 2, 512, 512], P('mp', 'dp'), as said below
- block_owner: int32 [4, 10], P('mp'), may hold values from 0 to 7, as said below
Outputs:
- directions: bfloat16 [40, 512, 512], P('mp')
- next_state: float32 [4, 8, 2, 2, 512, 512], P('mp', 'dp')
The draws below stay inside these ranges and needn't reach their ends.
Inputs may be any that keep to these rules, and one draw needn't show every extreme that they name: `block_owner`: within one row (one index of mp) no owner appears more than 2 times, and some owner appears exactly 2 times. Every index of dp owns some block. `factor_state`: every factor matrix is symmetric positive definite.
All inputs are finite; a program needn't handle non-finite values.
Results may differ from the reference program's by a relative error of at most 0.0004.
Values may be sent and summed in bfloat16 or wider, within the bound.
A program may use at most 128 MiB of HBM per device.

```python
import jax
import jax.numpy as jnp
from jax import lax

BS = 512
BLK_MP = 10
SLOTS = 2
ITERS = 3
BLOCKS = 40
N_DP = 8
N_MP = 4


def draw_gradients(key, part):
    subkeys = jax.random.split(key, 3)
    positions = jnp.arange(BLOCKS, dtype=jnp.float32) / max(BLOCKS - 1, 1)
    row_scale = jnp.exp(jax.random.uniform(subkeys[0], (BLOCKS, BS), jnp.float32, -0.6931, 0.6931))
    column_scale = jnp.exp(jax.random.uniform(subkeys[1], (BLOCKS, BS), jnp.float32, -0.6931, 0.6931))
    array_shape = (N_DP, BLOCKS, BS, BS)
    noise = jax.random.normal(subkeys[2], array_shape, jnp.float32)
    block_scale = 4.0 ** positions
    values = 0.2 * noise * block_scale[None, :, None, None] * row_scale[None, :, :, None] * column_scale[None, :, None, :]
    return jnp.clip(values, -16.0, 16.0).astype(jnp.bfloat16)


def draw_factor_state(key, part):
    first, second = jax.random.split(key)
    array_shape = (N_MP, N_DP, SLOTS, 2, BS, BS)
    basis = jax.random.normal(first, array_shape, jnp.float32)
    weights = jnp.exp(jax.random.uniform(second, array_shape[:-1], jnp.float32, -0.6931, 1.3863))
    gram = jnp.einsum('abcdik,abcdjk->abcdij', basis, basis) * (2.0 / BS)
    return gram + weights[..., None] * jnp.eye(BS, dtype=jnp.float32)


def owner_row(key, ranking, row_index):
    start = row_index * (BLK_MP - 1)
    steps = jnp.arange(BLK_MP, dtype=jnp.int32)
    if BLK_MP > N_DP:
        picks = (start + steps) % N_DP
    else:
        picks = (start + jnp.where(steps == BLK_MP - 1, 0, steps)) % N_DP
    listed = ranking[picks].astype(jnp.int32)
    arrangement = jax.random.permutation(key, BLK_MP)
    return listed[arrangement]


def draw_block_owner(key, part):
    ranking = jax.random.permutation(jax.random.fold_in(key, 7001), N_DP).astype(jnp.int32)
    rows = [owner_row(jax.random.fold_in(key, row_index), ranking, row_index) for row_index in range(N_MP)]
    return jnp.stack(rows)


def setup_inputs(seed: int = 0) -> dict:
    splits = jax.random.split(jax.random.key(seed), 4)
    gradients = draw_gradients(jax.random.fold_in(splits[3], 71), 0)
    factor_state = draw_factor_state(jax.random.fold_in(splits[3], 71), 0)
    block_owner = draw_block_owner(jax.random.fold_in(splits[3], 71), 0)
    return dict(gradients=gradients, factor_state=factor_state, block_owner=block_owner)


decay_rate = 0.95
ridge_term = 0.001
tiny_offset = 1e-06

def product(left, right):
    return jnp.dot(left, right, precision=lax.Precision.HIGHEST)

def inverse_root(matrix):
    width_rows = matrix.shape[0]
    identity = jnp.eye(width_rows, dtype=matrix.dtype)
    shifted = matrix + ridge_term * identity
    level_norm = jnp.sqrt(jnp.sum(shifted * shifted))
    moving = shifted / level_norm
    result = identity * level_norm ** (-0.25)
    for turn_index in range(ITERS):
        factor = (5.0 * identity - moving) * 0.25
        result = product(result, factor)
        if turn_index + 1 < ITERS:
            square = product(factor, factor)
            fourth = product(square, square)
            moving = product(fourth, moving)
    return result

def grafted(gradient, left_root, right_root):
    precond = product(product(left_root, gradient), right_root)
    target = jnp.sqrt(jnp.mean(gradient * gradient) + tiny_offset)
    actual = jnp.sqrt(jnp.mean(precond * precond) + tiny_offset)
    return precond * (target / actual)

def owner_slots(owners):
    block_count = owners.shape[0]
    positions = jnp.arange(block_count, dtype=jnp.int32)
    same_owner = owners[:, None] == owners[None, :]
    earlier = positions[None, :] < positions[:, None]
    return lax.optimization_barrier(jnp.sum((same_owner & earlier).astype(jnp.int32), axis=1))

def reference(gradients, factor_state, block_owner):

    def accumulate(replica, running):
        return running + gradients[replica].astype(running.dtype)
    summed = lax.fori_loop(0, gradients.shape[0], accumulate, jnp.zeros(gradients.shape[1:], jnp.float32))
    clip_value = 1.0 / jnp.sqrt(jnp.mean(summed * summed) + tiny_offset)
    clipped = summed * clip_value
    mp_index = jnp.arange(BLOCKS, dtype=jnp.int32) // BLK_MP
    owners = block_owner.reshape(-1).astype(jnp.int32)
    slot_of = jax.vmap(owner_slots)(block_owner).reshape(-1).astype(jnp.int32)
    old_pairs = factor_state[mp_index, owners, slot_of]

    def one_block(items):
        gradient, old_pair = items
        left = decay_rate * old_pair[0] + (1.0 - decay_rate) * product(gradient, gradient.T)
        right = decay_rate * old_pair[1] + (1.0 - decay_rate) * product(gradient.T, gradient)
        direction = grafted(gradient, inverse_root(left), inverse_root(right)).astype(jnp.bfloat16)
        return (direction, jnp.stack([left, right]))
    directions, pairs = lax.map(one_block, (clipped, old_pairs))
    next_state = factor_state.at[mp_index, owners, slot_of].set(pairs)
    return (directions, next_state)
```

```python
import functools

import jax
import jax.numpy as jnp
from jax import lax
from jax.experimental import pallas as pl
from jax.experimental.pallas import tpu as pltpu
from jax.sharding import PartitionSpec as P

ITERS = 3

decay_rate = 0.95
ridge_term = 0.001
tiny_offset = 1e-06

MESH = pl.DeviceIdType.MESH


def halves(value):
    high = value.astype(jnp.bfloat16)
    return high, (value - high.astype(jnp.float32)).astype(jnp.bfloat16)


def split_dot(left, right, dims=(1, 0)):
    def dot(a, b):
        return lax.dot_general(
            a, b, (((dims[0],), (dims[1],)), ((), ())), preferred_element_type=jnp.float32
        )
    return (dot(left[1], right[0]) + dot(left[0], right[1])) + dot(left[0], right[0])


def total_of(value):
    return jnp.sum(jnp.sum(value, axis=0, keepdims=True), axis=1, keepdims=True)


def inverse_root(matrix):
    width = matrix.shape[0]
    rows = lax.broadcasted_iota(jnp.int32, (width, width), 0)
    columns = lax.broadcasted_iota(jnp.int32, (width, width), 1)
    diagonal = rows == columns
    shifted = matrix + jnp.where(diagonal, ridge_term, 0.0)
    level_norm = jnp.sqrt(total_of(shifted * shifted))
    moving = shifted / level_norm
    result = None
    for turn in range(ITERS):
        factor = jnp.where(diagonal, 1.25, 0.0) - 0.25 * moving
        pair = halves(factor)
        result = factor if result is None else split_dot(halves(result), pair)
        if turn + 1 < ITERS:
            square = halves(split_dot(pair, pair))
            fourth = halves(split_dot(square, square))
            moving = split_dot(fourth, halves(moving))
    return result * (1.0 / jnp.sqrt(jnp.sqrt(level_norm)))


def step_kernel(n, n_mp, entries, keep_ref, sent_ref, state_ref, gathered_ref, next_ref,
                own, landed, summed, roots, finished, part, parts, row_part, row_parts,
                own_sem, send_sem, recv_sem, part_send, part_recv, row_send, row_recv,
                place_sem, out_send, out_recv, pair_send, pair_recv):
    me, mp = lax.axis_index("dp"), lax.axis_index("mp")
    slots, width = own.shape[0], own.shape[1]
    peers = [(k, lax.rem(me + k, n)) for k in range(1, n)]
    rows = [(k, lax.rem(mp + k, n_mp)) for k in range(1, n_mp)]

    barrier = pltpu.get_barrier_semaphore()
    for _, peer in peers:
        pl.semaphore_signal(barrier, inc=1, device_id=(peer, mp), device_id_type=MESH)
    for _, peer in rows:
        pl.semaphore_signal(barrier, inc=1, device_id=(me, peer), device_id_type=MESH)
    pl.semaphore_wait(barrier, n - 1 + n_mp - 1)

    copies = []
    for s in range(slots):
        group = []
        for k, peer in peers:
            copy = pltpu.make_async_remote_copy(
                src_ref=sent_ref.at[peer, s], dst_ref=landed.at[s, k - 1],
                send_sem=send_sem.at[s, k - 1], recv_sem=recv_sem.at[s, k - 1],
                device_id=(peer, mp), device_id_type=MESH)
            copy.start()
            group.append(copy)
        local = pltpu.make_async_copy(sent_ref.at[me, s], own.at[s], own_sem.at[s])
        local.start()
        copies.append((group, local))

    chunk = 64
    squares = []
    for s in range(slots):
        group, local = copies[s]
        local.wait()
        for copy in group:
            copy.wait_recv()

        def add(step, total):
            at = pl.ds(pl.multiple_of(step * chunk, chunk), chunk)
            value = own[s, at, :].astype(jnp.float32)
            for k in range(n - 1):
                value = value + landed[s, k, at, :].astype(jnp.float32)
            summed[s, at, :] = value
            return total + jnp.sum((value * value).reshape(chunk // 8, 8, width), axis=0)

        squares.append(total_of(lax.fori_loop(
            0, width // chunk, add, jnp.zeros((8, width), jnp.float32))))
        pair = halves(summed[s])
        next_ref[s, 0] = split_dot(pair, pair, (1, 1))
        next_ref[s, 1] = split_dot(pair, pair, (0, 0))

    part[...] = jnp.broadcast_to(functools.reduce(jnp.add, squares), part.shape)
    copies_part = []
    for k, peer in peers:
        copy = pltpu.make_async_remote_copy(
            src_ref=part, dst_ref=parts.at[k - 1], send_sem=part_send.at[k - 1],
            recv_sem=part_recv.at[k - 1], device_id=(peer, mp), device_id_type=MESH)
        copy.start()
        copies_part.append(copy)
    for copy in copies_part:
        copy.wait_recv()
    row_part[...] = part[...] + jnp.sum(parts[...], axis=0)
    copies_row = []
    for k, peer in rows:
        copy = pltpu.make_async_remote_copy(
            src_ref=row_part, dst_ref=row_parts.at[k - 1], send_sem=row_send.at[k - 1],
            recv_sem=row_recv.at[k - 1], device_id=(me, peer), device_id_type=MESH)
        copy.start()
        copies_row.append(copy)
    for copy in copies_row:
        copy.wait_recv()
    total = row_part[...] + jnp.sum(row_parts[...], axis=0)
    clip = (1.0 / jnp.sqrt(total / entries + tiny_offset))[:1, :1]

    core, pairs = lax.rem(me, 2), n // 2
    place = me // 2

    def out_copies(s):
        found = []
        for j in range(1, pairs):
            peer = lax.rem(place + j, pairs) * 2 + core
            found.append(pltpu.make_async_remote_copy(
                src_ref=finished.at[s], dst_ref=gathered_ref.at[me, s],
                send_sem=out_send.at[s, j], recv_sem=out_recv.at[s, j],
                device_id=(peer, mp), device_id_type=MESH))
        return found

    def pair_copy(s, j):
        source = lax.rem(place - j + pairs, pairs) * 2 + core
        return pltpu.make_async_remote_copy(
            src_ref=finished.at[s] if j == 0 else gathered_ref.at[source, s],
            dst_ref=gathered_ref.at[source, s],
            send_sem=pair_send.at[s, j], recv_sem=pair_recv.at[s, j],
            device_id=(me + 1 - 2 * core, mp), device_id_type=MESH)

    def place_copy(s):
        return pltpu.make_async_copy(finished.at[s], gathered_ref.at[me, s], place_sem.at[s])

    size = width * width
    for s in range(slots):

        def side_turn(side, carry):
            fresh = keep_ref[s] * state_ref[s, side] + (
                (1.0 - decay_rate) * clip * clip) * next_ref[s, side]
            next_ref[s, side] = fresh
            roots[side] = inverse_root(fresh)
            return carry

        lax.fori_loop(0, 2, side_turn, 0)
        gradient = summed[s] * clip
        precond = split_dot(halves(roots[0]), halves(gradient))
        precond = split_dot(halves(precond), halves(roots[1]))
        target = jnp.sqrt(squares[s] * clip * clip / size + tiny_offset)
        actual = jnp.sqrt(total_of(precond * precond) / size + tiny_offset)
        finished[s] = (precond * (target / actual)).astype(jnp.bfloat16)
        for copy in out_copies(s):
            copy.start()
        pair_copy(s, 0).start()
        place_copy(s).start()

    for s in range(slots):
        for j, copy in enumerate(out_copies(s)):
            copy.wait_recv()
            pair_copy(s, j + 1).start()
    for s in range(slots):
        for copy in out_copies(s):
            copy.wait_send()
        for j in range(pairs):
            pair_copy(s, j).wait()
        place_copy(s).wait()
        for copy in copies[s][0]:
            copy.wait_send()
    for copy in copies_part + copies_row:
        copy.wait_send()


def place_kernel(index_ref, valid_ref, source_ref, target_ref):
    value = source_ref[...].astype(jnp.float32)
    valid = valid_ref[pl.program_id(0)] > 0
    target_ref[...] = jnp.where(valid, value, 0.0).astype(target_ref.dtype)


def placed(source, index, valid):
    count, shape = index.shape[0], source.shape[1:]
    moved = 2 * count * shape[0] * shape[1] * source.dtype.itemsize
    return pl.pallas_call(
        place_kernel,
        out_shape=jax.ShapeDtypeStruct((count,) + shape, source.dtype),
        grid_spec=pltpu.PrefetchScalarGridSpec(
            num_scalar_prefetch=2, grid=(count,),
            in_specs=[pl.BlockSpec((1,) + shape, lambda i, index, valid: (index[i], 0, 0))],
            out_specs=pl.BlockSpec((1,) + shape, lambda i, index, valid: (i, 0, 0))),
        cost_estimate=pl.CostEstimate(flops=0, bytes_accessed=moved, transcendentals=0),
    )(index, valid, source)


def owner_slots(owners):
    positions = jnp.arange(owners.shape[0], dtype=jnp.int32)
    same_owner = owners[:, None] == owners[None, :]
    earlier = positions[None, :] < positions[:, None]
    return jnp.sum((same_owner & earlier).astype(jnp.int32), axis=1)


def shards(n, n_mp, gradients, factor_state, block_owner):
    owners = block_owner[0]
    blocks, width = gradients.shape[1], gradients.shape[2]
    slots = factor_state.shape[2]
    slot_of = owner_slots(owners)
    positions = jnp.arange(blocks, dtype=jnp.int32)
    spot = owners * slots + slot_of
    hits = jnp.arange(n * slots, dtype=jnp.int32)[:, None] == spot[None, :]
    occupied = jnp.any(hits, axis=1)
    block_at = jnp.sum(jnp.where(hits, positions[None, :], 0), axis=1)
    sent = placed(gradients[0], block_at, occupied.astype(jnp.int32))
    sent = sent.reshape(n, slots, width, width)
    mine = lax.dynamic_slice_in_dim(occupied, lax.axis_index("dp") * slots, slots)
    keep = jnp.where(mine, decay_rate, 1.0).astype(jnp.float32)

    vmem, sem = pltpu.VMEM, pltpu.SemaphoreType.DMA
    f32, bf16 = jnp.float32, jnp.bfloat16
    entries = float(blocks * n_mp * width * width)
    pairs = n // 2
    gathered, fresh = pl.pallas_call(
        functools.partial(step_kernel, n, n_mp, entries),
        out_shape=(jax.ShapeDtypeStruct((n, slots, width, width), bf16),
                   jax.ShapeDtypeStruct(factor_state.shape[2:], f32)),
        in_specs=[pl.BlockSpec(memory_space=pltpu.SMEM), pl.BlockSpec(memory_space=pl.ANY),
                  pl.BlockSpec(memory_space=vmem)],
        out_specs=(pl.BlockSpec(memory_space=pl.ANY), pl.BlockSpec(memory_space=vmem)),
        scratch_shapes=[
            vmem((slots, width, width), bf16), vmem((slots, n - 1, width, width), bf16),
            vmem((slots, width, width), f32), vmem((2, width, width), f32),
            vmem((slots, width, width), bf16),
            vmem((8, 128), f32), vmem((n - 1, 8, 128), f32),
            vmem((8, 128), f32), vmem((n_mp - 1, 8, 128), f32),
            sem((slots,)), sem((slots, n - 1)), sem((slots, n - 1)),
            sem((n - 1,)), sem((n - 1,)), sem((n_mp - 1,)), sem((n_mp - 1,)),
            sem((slots,)), sem((slots, pairs)), sem((slots, pairs)),
            sem((slots, pairs)), sem((slots, pairs))],
        compiler_params=pltpu.CompilerParams(
            collective_id=0, has_side_effects=True, vmem_limit_bytes=62 * 1024 * 1024),
    )(keep, sent, factor_state[0, 0])
    directions = placed(
        gathered.reshape(n * slots, width, width), spot, jnp.ones((blocks,), jnp.int32))
    return (directions, fresh[None, None])


def solution(mesh):
    in_specs = (P("dp", "mp", None, None), P("mp", "dp", None, None, None, None), P("mp", None))
    out_specs = (P("mp", None, None), P("mp", "dp", None, None, None, None))
    body = functools.partial(shards, mesh.shape["dp"], mesh.shape["mp"])
    return jax.shard_map(body, mesh=mesh, in_specs=in_specs, out_specs=out_specs, check_vma=False)
```

```python
import functools

import jax
import jax.numpy as jnp
from jax import lax
from jax.experimental import pallas as pl
from jax.experimental.pallas import tpu as pltpu
from jax.sharding import PartitionSpec as P

ITERS = 3

decay_rate = 0.95
ridge_term = 0.001
tiny_offset = 1e-06

MESH = pl.DeviceIdType.MESH


def halves(value):
    high = value.astype(jnp.bfloat16)
    return high, (value - high.astype(jnp.float32)).astype(jnp.bfloat16)


def split_dot(left, right, dims=(1, 0)):
    def dot(a, b):
        return lax.dot_general(
            a, b, (((dims[0],), (dims[1],)), ((), ())), preferred_element_type=jnp.float32
        )
    return (dot(left[1], right[0]) + dot(left[0], right[1])) + dot(left[0], right[0])


def total_of(value):
    return jnp.sum(jnp.sum(value, axis=0, keepdims=True), axis=1, keepdims=True)


def inverse_root(matrix):
    width = matrix.shape[0]
    rows = lax.broadcasted_iota(jnp.int32, (width, width), 0)
    columns = lax.broadcasted_iota(jnp.int32, (width, width), 1)
    diagonal = rows == columns
    shifted = matrix + jnp.where(diagonal, ridge_term, 0.0)
    level_norm = jnp.sqrt(total_of(shifted * shifted))
    moving = shifted / level_norm
    result = None
    for turn in range(ITERS):
        factor = jnp.where(diagonal, 1.25, 0.0) - 0.25 * moving
        pair = halves(factor)
        result = factor if result is None else split_dot(halves(result), pair)
        if turn + 1 < ITERS:
            square = halves(split_dot(pair, pair))
            fourth = halves(split_dot(square, square))
            moving = split_dot(fourth, halves(moving))
    return result * (1.0 / jnp.sqrt(jnp.sqrt(level_norm)))


def step_kernel(n, n_mp, entries, keep_ref, sent_ref, state_ref, gathered_ref, next_ref,
                own, landed, summed, roots, finished, part, parts, row_part, row_parts,
                own_sem, send_sem, recv_sem, part_send, part_recv, row_send, row_recv,
                place_sem, out_send, out_recv, pair_send, pair_recv):
    me, mp = lax.axis_index("dp"), lax.axis_index("mp")
    slots, width = own.shape[0], own.shape[1]
    peers = [(k, lax.rem(me + k, n)) for k in range(1, n)]
    rows = [(k, lax.rem(mp + k, n_mp)) for k in range(1, n_mp)]

    barrier = pltpu.get_barrier_semaphore()
    for _, peer in peers:
        pl.semaphore_signal(barrier, inc=1, device_id=(peer, mp), device_id_type=MESH)
    for _, peer in rows:
        pl.semaphore_signal(barrier, inc=1, device_id=(me, peer), device_id_type=MESH)
    pl.semaphore_wait(barrier, n - 1 + n_mp - 1)

    copies = []
    for s in range(slots):
        group = []
        for k, peer in peers:
            copy = pltpu.make_async_remote_copy(
                src_ref=sent_ref.at[peer, s], dst_ref=landed.at[s, k - 1],
                send_sem=send_sem.at[s, k - 1], recv_sem=recv_sem.at[s, k - 1],
                device_id=(peer, mp), device_id_type=MESH)
            copy.start()
            group.append(copy)
        local = pltpu.make_async_copy(sent_ref.at[me, s], own.at[s], own_sem.at[s])
        local.start()
        copies.append((group, local))

    chunk = 64
    squares = []
    for s in range(slots):
        group, local = copies[s]
        local.wait()
        for copy in group:
            copy.wait_recv()

        def add(step, total):
            at = pl.ds(pl.multiple_of(step * chunk, chunk), chunk)
            value = own[s, at, :].astype(jnp.float32)
            for k in range(n - 1):
                value = value + landed[s, k, at, :].astype(jnp.float32)
            summed[s, at, :] = value
            return total + jnp.sum((value * value).reshape(chunk // 8, 8, width), axis=0)

        squares.append(total_of(lax.fori_loop(
            0, width // chunk, add, jnp.zeros((8, width), jnp.float32))))
        pair = halves(summed[s])
        next_ref[s, 0] = split_dot(pair, pair, (1, 1))
        next_ref[s, 1] = split_dot(pair, pair, (0, 0))

    part[...] = jnp.broadcast_to(functools.reduce(jnp.add, squares), part.shape)
    copies_part = []
    for k, peer in peers:
        copy = pltpu.make_async_remote_copy(
            src_ref=part, dst_ref=parts.at[k - 1], send_sem=part_send.at[k - 1],
            recv_sem=part_recv.at[k - 1], device_id=(peer, mp), device_id_type=MESH)
        copy.start()
        copies_part.append(copy)
    for copy in copies_part:
        copy.wait_recv()
    row_part[...] = part[...] + jnp.sum(parts[...], axis=0)
    copies_row = []
    for k, peer in rows:
        copy = pltpu.make_async_remote_copy(
            src_ref=row_part, dst_ref=row_parts.at[k - 1], send_sem=row_send.at[k - 1],
            recv_sem=row_recv.at[k - 1], device_id=(me, peer), device_id_type=MESH)
        copy.start()
        copies_row.append(copy)
    for copy in copies_row:
        copy.wait_recv()
    total = row_part[...] + jnp.sum(row_parts[...], axis=0)
    clip = (1.0 / jnp.sqrt(total / entries + tiny_offset))[:1, :1]

    core, pairs = lax.rem(me, 2), n // 2
    place = me // 2

    def out_copies(s):
        found = []
        for j in range(1, pairs):
            peer = lax.rem(place + j, pairs) * 2 + core
            found.append(pltpu.make_async_remote_copy(
                src_ref=finished.at[s], dst_ref=gathered_ref.at[me, s],
                send_sem=out_send.at[s, j], recv_sem=out_recv.at[s, j],
                device_id=(peer, mp), device_id_type=MESH))
        return found

    def pair_copy(s, j):
        source = lax.rem(place - j + pairs, pairs) * 2 + core
        return pltpu.make_async_remote_copy(
            src_ref=finished.at[s] if j == 0 else gathered_ref.at[source, s],
            dst_ref=gathered_ref.at[source, s],
            send_sem=pair_send.at[s, j], recv_sem=pair_recv.at[s, j],
            device_id=(me + 1 - 2 * core, mp), device_id_type=MESH)

    def place_copy(s):
        return pltpu.make_async_copy(finished.at[s], gathered_ref.at[me, s], place_sem.at[s])

    size = width * width
    for s in range(slots):

        def side_turn(side, carry):
            fresh = keep_ref[s] * state_ref[s, side] + (
                (1.0 - decay_rate) * clip * clip) * next_ref[s, side]
            next_ref[s, side] = fresh
            roots[side] = inverse_root(fresh)
            return carry

        lax.fori_loop(0, 2, side_turn, 0)
        gradient = summed[s] * clip
        precond = split_dot(halves(roots[0]), halves(gradient))
        precond = split_dot(halves(precond), halves(roots[1]))
        target = jnp.sqrt(squares[s] * clip * clip / size + tiny_offset)
        actual = jnp.sqrt(total_of(precond * precond) / size + tiny_offset)
        finished[s] = (precond * (target / actual)).astype(jnp.bfloat16)
        for copy in out_copies(s):
            copy.start()
        pair_copy(s, 0).start()
        place_copy(s).start()

    for s in range(slots):
        for j, copy in enumerate(out_copies(s)):
            copy.wait_recv()
            pair_copy(s, j + 1).start()
    for s in range(slots):
        for copy in out_copies(s):
            copy.wait_send()
        for j in range(pairs):
            pair_copy(s, j).wait()
        place_copy(s).wait()
        for copy in copies[s][0]:
            copy.wait_send()
    for copy in copies_part + copies_row:
        copy.wait_send()


def place_kernel(index_ref, valid_ref, source_ref, target_ref):
    valid = valid_ref[pl.program_id(0)] > 0

    @pl.when(valid)
    def _():
        target_ref[...] = source_ref[...]

    @pl.when(jnp.logical_not(valid))
    def _():
        target_ref[...] = jnp.zeros_like(target_ref)


def placed(source, index, valid):
    count, shape = index.shape[0], source.shape[1:]
    moved = 2 * count * shape[0] * shape[1] * source.dtype.itemsize
    return pl.pallas_call(
        place_kernel,
        out_shape=jax.ShapeDtypeStruct((count,) + shape, source.dtype),
        grid_spec=pltpu.PrefetchScalarGridSpec(
            num_scalar_prefetch=2, grid=(count,),
            in_specs=[pl.BlockSpec((1,) + shape, lambda i, index, valid: (index[i], 0, 0))],
            out_specs=pl.BlockSpec((1,) + shape, lambda i, index, valid: (i, 0, 0))),
        cost_estimate=pl.CostEstimate(flops=0, bytes_accessed=moved, transcendentals=0),
    )(index, valid, source)


def owner_slots(owners):
    positions = jnp.arange(owners.shape[0], dtype=jnp.int32)
    same_owner = owners[:, None] == owners[None, :]
    earlier = positions[None, :] < positions[:, None]
    return jnp.sum((same_owner & earlier).astype(jnp.int32), axis=1)


def shards(n, n_mp, gradients, factor_state, block_owner):
    owners = block_owner[0]
    blocks, width = gradients.shape[1], gradients.shape[2]
    slots = factor_state.shape[2]
    slot_of = owner_slots(owners)
    positions = jnp.arange(blocks, dtype=jnp.int32)
    spot = owners * slots + slot_of
    hits = jnp.arange(n * slots, dtype=jnp.int32)[:, None] == spot[None, :]
    occupied = jnp.any(hits, axis=1)
    block_at = jnp.sum(jnp.where(hits, positions[None, :], 0), axis=1)
    sent = placed(gradients[0], block_at, occupied.astype(jnp.int32))
    sent = sent.reshape(n, slots, width, width)
    mine = lax.dynamic_slice_in_dim(occupied, lax.axis_index("dp") * slots, slots)
    keep = jnp.where(mine, decay_rate, 1.0).astype(jnp.float32)

    vmem, sem = pltpu.VMEM, pltpu.SemaphoreType.DMA
    f32, bf16 = jnp.float32, jnp.bfloat16
    entries = float(blocks * n_mp * width * width)
    pairs = n // 2
    gathered, fresh = pl.pallas_call(
        functools.partial(step_kernel, n, n_mp, entries),
        out_shape=(jax.ShapeDtypeStruct((n, slots, width, width), bf16),
                   jax.ShapeDtypeStruct(factor_state.shape[2:], f32)),
        in_specs=[pl.BlockSpec(memory_space=pltpu.SMEM), pl.BlockSpec(memory_space=pl.ANY),
                  pl.BlockSpec(memory_space=vmem)],
        out_specs=(pl.BlockSpec(memory_space=pl.ANY), pl.BlockSpec(memory_space=vmem)),
        scratch_shapes=[
            vmem((slots, width, width), bf16), vmem((slots, n - 1, width, width), bf16),
            vmem((slots, width, width), f32), vmem((2, width, width), f32),
            vmem((slots, width, width), bf16),
            vmem((8, 128), f32), vmem((n - 1, 8, 128), f32),
            vmem((8, 128), f32), vmem((n_mp - 1, 8, 128), f32),
            sem((slots,)), sem((slots, n - 1)), sem((slots, n - 1)),
            sem((n - 1,)), sem((n - 1,)), sem((n_mp - 1,)), sem((n_mp - 1,)),
            sem((slots,)), sem((slots, pairs)), sem((slots, pairs)),
            sem((slots, pairs)), sem((slots, pairs))],
        compiler_params=pltpu.CompilerParams(
            collective_id=0, has_side_effects=True, vmem_limit_bytes=62 * 1024 * 1024),
    )(keep, sent, factor_state[0, 0])
    directions = placed(
        gathered.reshape(n * slots, width, width), spot, jnp.ones((blocks,), jnp.int32))
    return (directions, fresh[None, None])


def solution(mesh):
    in_specs = (P("dp", "mp", None, None), P("mp", "dp", None, None, None, None), P("mp", None))
    out_specs = (P("mp", None, None), P("mp", "dp", None, None, None, None))
    body = functools.partial(shards, mesh.shape["dp"], mesh.shape["mp"])
    return jax.shard_map(body, mesh=mesh, in_specs=in_specs, out_specs=out_specs, check_vma=False)
```

```python
import functools

import jax
import jax.numpy as jnp
from jax import lax
from jax.experimental import pallas as pl
from jax.experimental.pallas import tpu as pltpu
from jax.sharding import PartitionSpec as P

ITERS = 3

decay_rate = 0.95
ridge_term = 0.001
tiny_offset = 1e-06

MESH = pl.DeviceIdType.MESH


def halves(value):
    high = value.astype(jnp.bfloat16)
    return high, (value - high.astype(jnp.float32)).astype(jnp.bfloat16)


def split_dot(left, right, dims=(1, 0)):
    def dot(a, b):
        return lax.dot_general(
            a, b, (((dims[0],), (dims[1],)), ((), ())), preferred_element_type=jnp.float32
        )
    return (dot(left[1], right[0]) + dot(left[0], right[1])) + dot(left[0], right[0])


def total_of(value):
    return jnp.sum(jnp.sum(value, axis=0, keepdims=True), axis=1, keepdims=True)


def inverse_roots(matrices):
    width = matrices[0].shape[0]
    rows = lax.broadcasted_iota(jnp.int32, (width, width), 0)
    columns = lax.broadcasted_iota(jnp.int32, (width, width), 1)
    diagonal = rows == columns
    shifted = [matrix + jnp.where(diagonal, ridge_term, 0.0) for matrix in matrices]
    level_norm = [jnp.sqrt(total_of(each * each)) for each in shifted]
    moving = [each / norm for each, norm in zip(shifted, level_norm)]
    result = None
    for turn in range(ITERS):
        factor = [jnp.where(diagonal, 1.25, 0.0) - 0.25 * each for each in moving]
        pair = [halves(each) for each in factor]
        if result is None:
            result = factor
        else:
            result = [split_dot(halves(x), p) for x, p in zip(result, pair)]
        if turn + 1 < ITERS:
            square = [halves(split_dot(p, p)) for p in pair]
            fourth = [halves(split_dot(q, q)) for q in square]
            moving = [split_dot(f, halves(m)) for f, m in zip(fourth, moving)]
    return [x * (1.0 / jnp.sqrt(jnp.sqrt(norm))) for x, norm in zip(result, level_norm)]


def step_kernel(n, n_mp, entries, keep_ref, sent_ref, state_ref, gathered_ref, next_ref,
                own, landed, summed, finished, part, parts, row_part, row_parts,
                own_sem, send_sem, recv_sem, part_send, part_recv, row_send, row_recv,
                place_sem, out_send, out_recv, pair_send, pair_recv):
    me, mp = lax.axis_index("dp"), lax.axis_index("mp")
    slots, width = own.shape[0], own.shape[1]
    peers = [(k, lax.rem(me + k, n)) for k in range(1, n)]
    rows = [(k, lax.rem(mp + k, n_mp)) for k in range(1, n_mp)]

    barrier = pltpu.get_barrier_semaphore()
    for _, peer in peers:
        pl.semaphore_signal(barrier, inc=1, device_id=(peer, mp), device_id_type=MESH)
    for _, peer in rows:
        pl.semaphore_signal(barrier, inc=1, device_id=(me, peer), device_id_type=MESH)
    pl.semaphore_wait(barrier, n - 1 + n_mp - 1)

    copies = []
    for s in range(slots):
        group = []
        for k, peer in peers:
            copy = pltpu.make_async_remote_copy(
                src_ref=sent_ref.at[peer, s], dst_ref=landed.at[s, k - 1],
                send_sem=send_sem.at[s, k - 1], recv_sem=recv_sem.at[s, k - 1],
                device_id=(peer, mp), device_id_type=MESH)
            copy.start()
            group.append(copy)
        local = pltpu.make_async_copy(sent_ref.at[me, s], own.at[s], own_sem.at[s])
        local.start()
        copies.append((group, local))

    chunk = 64
    squares = []
    for s in range(slots):
        group, local = copies[s]
        local.wait()
        for copy in group:
            copy.wait_recv()

        def add(step, total):
            at = pl.ds(pl.multiple_of(step * chunk, chunk), chunk)
            value = own[s, at, :].astype(jnp.float32)
            for k in range(n - 1):
                value = value + landed[s, k, at, :].astype(jnp.float32)
            summed[s, at, :] = value
            return total + jnp.sum((value * value).reshape(chunk // 8, 8, width), axis=0)

        squares.append(total_of(lax.fori_loop(
            0, width // chunk, add, jnp.zeros((8, width), jnp.float32))))
        pair = halves(summed[s])
        next_ref[s, 0] = split_dot(pair, pair, (1, 1))
        next_ref[s, 1] = split_dot(pair, pair, (0, 0))

    part[...] = jnp.broadcast_to(functools.reduce(jnp.add, squares), part.shape)
    copies_part = []
    for k, peer in peers:
        copy = pltpu.make_async_remote_copy(
            src_ref=part, dst_ref=parts.at[k - 1], send_sem=part_send.at[k - 1],
            recv_sem=part_recv.at[k - 1], device_id=(peer, mp), device_id_type=MESH)
        copy.start()
        copies_part.append(copy)
    for copy in copies_part:
        copy.wait_recv()
    row_part[...] = part[...] + jnp.sum(parts[...], axis=0)
    copies_row = []
    for k, peer in rows:
        copy = pltpu.make_async_remote_copy(
            src_ref=row_part, dst_ref=row_parts.at[k - 1], send_sem=row_send.at[k - 1],
            recv_sem=row_recv.at[k - 1], device_id=(me, peer), device_id_type=MESH)
        copy.start()
        copies_row.append(copy)
    for copy in copies_row:
        copy.wait_recv()
    total = row_part[...] + jnp.sum(row_parts[...], axis=0)
    clip = (1.0 / jnp.sqrt(total / entries + tiny_offset))[:1, :1]

    core, pairs = lax.rem(me, 2), n // 2
    place = me // 2

    def out_copies(s):
        found = []
        for j in range(1, pairs):
            peer = lax.rem(place + j, pairs) * 2 + core
            found.append(pltpu.make_async_remote_copy(
                src_ref=finished.at[s], dst_ref=gathered_ref.at[me, s],
                send_sem=out_send.at[s, j], recv_sem=out_recv.at[s, j],
                device_id=(peer, mp), device_id_type=MESH))
        return found

    def pair_copy(s, j):
        source = lax.rem(place - j + pairs, pairs) * 2 + core
        return pltpu.make_async_remote_copy(
            src_ref=finished.at[s] if j == 0 else gathered_ref.at[source, s],
            dst_ref=gathered_ref.at[source, s],
            send_sem=pair_send.at[s, j], recv_sem=pair_recv.at[s, j],
            device_id=(me + 1 - 2 * core, mp), device_id_type=MESH)

    def place_copy(s):
        return pltpu.make_async_copy(finished.at[s], gathered_ref.at[me, s], place_sem.at[s])

    size = width * width
    for s in range(slots):

        sides = []
        for side in range(2):
            fresh = keep_ref[s] * state_ref[s, side] + (
                (1.0 - decay_rate) * clip * clip) * next_ref[s, side]
            next_ref[s, side] = fresh
            sides.append(fresh)
        left_root, right_root = inverse_roots(sides)
        gradient = summed[s] * clip
        precond = split_dot(halves(left_root), halves(gradient))
        precond = split_dot(halves(precond), halves(right_root))
        target = jnp.sqrt(squares[s] * clip * clip / size + tiny_offset)
        actual = jnp.sqrt(total_of(precond * precond) / size + tiny_offset)
        finished[s] = (precond * (target / actual)).astype(jnp.bfloat16)
        for copy in out_copies(s):
            copy.start()
        pair_copy(s, 0).start()
        place_copy(s).start()

    for s in range(slots):
        for j, copy in enumerate(out_copies(s)):
            copy.wait_recv()
            pair_copy(s, j + 1).start()
    for s in range(slots):
        for copy in out_copies(s):
            copy.wait_send()
        for j in range(pairs):
            pair_copy(s, j).wait()
        place_copy(s).wait()
        for copy in copies[s][0]:
            copy.wait_send()
    for copy in copies_part + copies_row:
        copy.wait_send()


def place_kernel(index_ref, valid_ref, source_ref, target_ref):
    valid = valid_ref[pl.program_id(0)] > 0

    @pl.when(valid)
    def _():
        target_ref[...] = source_ref[...]

    @pl.when(jnp.logical_not(valid))
    def _():
        target_ref[...] = jnp.zeros_like(target_ref)


def placed(source, index, valid):
    count, shape = index.shape[0], source.shape[1:]
    moved = 2 * count * shape[0] * shape[1] * source.dtype.itemsize
    return pl.pallas_call(
        place_kernel,
        out_shape=jax.ShapeDtypeStruct((count,) + shape, source.dtype),
        grid_spec=pltpu.PrefetchScalarGridSpec(
            num_scalar_prefetch=2, grid=(count,),
            in_specs=[pl.BlockSpec((1,) + shape, lambda i, index, valid: (index[i], 0, 0))],
            out_specs=pl.BlockSpec((1,) + shape, lambda i, index, valid: (i, 0, 0))),
        cost_estimate=pl.CostEstimate(flops=0, bytes_accessed=moved, transcendentals=0),
    )(index, valid, source)


def owner_slots(owners):
    positions = jnp.arange(owners.shape[0], dtype=jnp.int32)
    same_owner = owners[:, None] == owners[None, :]
    earlier = positions[None, :] < positions[:, None]
    return jnp.sum((same_owner & earlier).astype(jnp.int32), axis=1)


def shards(n, n_mp, gradients, factor_state, block_owner):
    owners = block_owner[0]
    blocks, width = gradients.shape[1], gradients.shape[2]
    slots = factor_state.shape[2]
    slot_of = owner_slots(owners)
    positions = jnp.arange(blocks, dtype=jnp.int32)
    spot = owners * slots + slot_of
    hits = jnp.arange(n * slots, dtype=jnp.int32)[:, None] == spot[None, :]
    occupied = jnp.any(hits, axis=1)
    block_at = jnp.sum(jnp.where(hits, positions[None, :], 0), axis=1)
    sent = placed(gradients[0], block_at, occupied.astype(jnp.int32))
    sent = sent.reshape(n, slots, width, width)
    mine = lax.dynamic_slice_in_dim(occupied, lax.axis_index("dp") * slots, slots)
    keep = jnp.where(mine, decay_rate, 1.0).astype(jnp.float32)

    vmem, sem = pltpu.VMEM, pltpu.SemaphoreType.DMA
    f32, bf16 = jnp.float32, jnp.bfloat16
    entries = float(blocks * n_mp * width * width)
    pairs = n // 2
    gathered, fresh = pl.pallas_call(
        functools.partial(step_kernel, n, n_mp, entries),
        out_shape=(jax.ShapeDtypeStruct((n, slots, width, width), bf16),
                   jax.ShapeDtypeStruct(factor_state.shape[2:], f32)),
        in_specs=[pl.BlockSpec(memory_space=pltpu.SMEM), pl.BlockSpec(memory_space=pl.ANY),
                  pl.BlockSpec(memory_space=vmem)],
        out_specs=(pl.BlockSpec(memory_space=pl.ANY), pl.BlockSpec(memory_space=vmem)),
        scratch_shapes=[
            vmem((slots, width, width), bf16), vmem((slots, n - 1, width, width), bf16),
            vmem((slots, width, width), f32),
            vmem((slots, width, width), bf16),
            vmem((8, 128), f32), vmem((n - 1, 8, 128), f32),
            vmem((8, 128), f32), vmem((n_mp - 1, 8, 128), f32),
            sem((slots,)), sem((slots, n - 1)), sem((slots, n - 1)),
            sem((n - 1,)), sem((n - 1,)), sem((n_mp - 1,)), sem((n_mp - 1,)),
            sem((slots,)), sem((slots, pairs)), sem((slots, pairs)),
            sem((slots, pairs)), sem((slots, pairs))],
        compiler_params=pltpu.CompilerParams(
            collective_id=0, has_side_effects=True, vmem_limit_bytes=62 * 1024 * 1024),
    )(keep, sent, factor_state[0, 0])
    directions = placed(
        gathered.reshape(n * slots, width, width), spot, jnp.ones((blocks,), jnp.int32))
    return (directions, fresh[None, None])


def solution(mesh):
    in_specs = (P("dp", "mp", None, None), P("mp", "dp", None, None, None, None), P("mp", None))
    out_specs = (P("mp", None, None), P("mp", "dp", None, None, None, None))
    body = functools.partial(shards, mesh.shape["dp"], mesh.shape["mp"])
    return jax.shard_map(body, mesh=mesh, in_specs=in_specs, out_specs=out_specs, check_vma=False)
```
